32 devices in a mesh: band: 8 (over z, x), mem: 4 (over y, core).
Axes of the slice: x: 2, y: 2, z: 4, core: 2. Of those that a mesh axis runs over, the one named last changes fastest.
Arguments:
- coef: float32 [2, 512, 128, 2, 512], P(None, 'band', 'mem'), may hold values from -6 to 6
- perturb: bfloat16 [768, 128, 2, 1536], P('band', 'mem'), may hold values from -6 to 6
- weight: float32 [768, 2, 1536], P('band'), may hold values from 1 to 10
- table: bfloat16 [512, 512, 768], P('band'), may hold values from -0.0078125 to 0.0078125
- wave_map: int32 [512], replicated, may hold values from 0 to 511, each once
- lat_map: int32 [768], replicated, may hold values from 0 to 767, each once
Outputs:
- increment: float32 [768, 2, 1536], P('band')
- product: float32 [2, 512, 128, 2, 512], P(None, 'band', 'mem')
The draws below stay inside these ranges and needn't reach their ends.
Inputs may be any that keep to these rules, and one draw needn't show every extreme that they name: A permutation: spectral row r holds zonal wavenumber wave_map[r]. A permutation: grid row s holds Gaussian latitude lat_map[s]; the last dimension of table stands in natural latitude order.
All inputs are finite; a program needn't handle non-finite values.
Results may differ from the reference program's by a relative error of at most 0.0048.
Values may be sent and summed in bfloat16 or wider, within the bound.
No kernel may reach another device: no remote copies, remote signals or barrier semaphores. Data moves between devices by JAX's collectives and lax.ppermute only.
A program may use at most 320 MiB of HBM per device.

```python
import math
import jax
import jax.numpy as jnp
from jax import lax

M = 512
LAT = 768
LON = 1536
LEV = 2
MEMBERS = 128


def block_scale(stream_key, extent, split, smallest, largest):
    def one(position, blocks):
        draws = jax.random.uniform(jax.random.fold_in(jax.random.fold_in(stream_key, 6), position), (blocks,), jnp.float32, smallest / len(split), largest / len(split))
        return jnp.repeat(jnp.exp(draws), extent[position] // blocks).reshape((-1,) + (1,) * (len(extent) - position - 1))

    gain = one(*split[0])
    for cut in split[1:]:
        gain = gain * one(*cut)
    return gain


def noise(rng, shape, deviation, bound, pieces=(), held_as=jnp.bfloat16):
    result = jax.random.normal(rng, shape, jnp.float32) * deviation
    if len(pieces) > 0:
        result = block_scale(rng, shape, pieces, -0.22, 0.18) * result
    return jnp.clip(result, min=-bound, max=bound).astype(held_as)


def setup_inputs(seed: int = 0) -> dict:
    seeds = jax.random.split(jax.random.key(seed), 7)
    return {
        "coef": noise(seeds[0], (2, M, MEMBERS, LEV, M), 1.0, 6.0, ((1, 8), (2, 4)), jnp.float32),
        "perturb": noise(seeds[1], (LAT, MEMBERS, LEV, LON), 1.0, 6.0, ((0, 8), (1, 4))),
        "weight": jnp.clip(jnp.exp(math.log(10.0) - 2.3025851 * jax.random.uniform(seeds[2], (LAT, LEV, LON), jnp.float32) ** block_scale(seeds[2], (LAT, LEV, LON), ((0, 8),), -0.2, 0.2)), 1.0, 10.0),
        "table": noise(seeds[3], (M, M, LAT), (2 * M * M) ** -0.5, 0.0078125, ((0, 8),)),
        "wave_map": jax.random.permutation(seeds[4], M).astype(jnp.int32),
        "lat_map": jax.random.permutation(seeds[5], LAT).astype(jnp.int32),
    }


def make_tables(table, wave_map, lat_map, lon):
    nwave = table.shape[1]
    start_offsets = jnp.arange(nwave, dtype=jnp.int32)
    valid = (start_offsets[None, :] < (nwave - wave_map)[:, None]).astype(jnp.float32)
    loc_table = (jnp.take(table, lat_map, axis=2).astype(jnp.float32) * valid[:, :, None]).astype(jnp.bfloat16)
    columns = jnp.arange(lon, dtype=jnp.int32)
    phase = wave_map[:, None] * columns[None, :] % lon
    angle = phase.astype(jnp.float32) * (2.0 * math.pi / lon)
    scale_multiplier = jnp.where(wave_map == 0, 1.0, 2.0).astype(jnp.float32)[:, None]
    fourier_table = jnp.stack([scale_multiplier * jnp.cos(angle), -scale_multiplier * jnp.sin(angle)], axis=0).astype(jnp.bfloat16)
    return (valid, loc_table, fourier_table)

def reference(coef, perturb, weight, table, wave_map, lat_map):
    ensemble_members = coef.shape[2]
    lon = perturb.shape[-1]
    valid, loc_table, fourier_table = make_tables(table, wave_map, lat_map, lon)
    scale = 1.0 / math.sqrt(ensemble_members - 1)
    masked = coef * valid[None, :, None, None, :]
    spec = masked.astype(jnp.bfloat16)
    fields = jnp.einsum('crklj,rjs->crskl', spec.astype(jnp.float32), loc_table.astype(jnp.float32)).astype(jnp.bfloat16)
    grid = jnp.einsum('crskl,crx->sklx', fields.astype(jnp.float32), fourier_table.astype(jnp.float32))
    increment = lax.optimization_barrier(jnp.sum(perturb.astype(jnp.float32) * grid, axis=1)) * scale
    gradient = weight * increment
    adjoint_grid = (perturb.astype(jnp.float32) * gradient[:, None] * scale).astype(jnp.bfloat16)
    adjoint_fields = jnp.einsum('sklx,crx->crskl', adjoint_grid.astype(jnp.float32), fourier_table.astype(jnp.float32)).astype(jnp.bfloat16)
    back = jnp.einsum('crskl,rjs->crklj', adjoint_fields.astype(jnp.float32), loc_table.astype(jnp.float32))
    product = masked + back
    return (increment, product)
```

```python
import functools
import math

import jax
import jax.numpy as jnp
from jax import lax
from jax.experimental import pallas as pl
from jax.experimental.pallas import tpu as pltpu
from jax.sharding import PartitionSpec as P

F32 = jnp.float32
BF16 = jnp.bfloat16
VMEM_LIMIT = 56 * 2**20


def dot(a, b, ca, cb):
    return lax.dot_general(a, b, (((ca,), (cb,)), ((), ())), preferred_element_type=F32)


def divisor(n, most):
    return next(d for d in range(min(n, most), 0, -1) if n % d == 0)


def level_rows(ref, i):
    parts, _, _, levels, _ = ref.shape
    return jnp.concatenate(
        [ref[c, i, :, l, :] for c in range(parts) for l in range(levels)], axis=0
    )


def masked(full, wave):
    offset = lax.broadcasted_iota(jnp.int32, full.shape, 1)
    return jnp.where(offset < full.shape[1] - wave, full, 0.0)


def synth_kernel(first, rb, pair, waves, coef, table, spread, out, work):
    block, inner = pl.program_id(0), pl.program_id(1)
    ns = spread.shape[0]
    fields = []
    for i in range(pair):
        wave = waves[first + block * rb + inner * pair + i]
        spec = masked(level_rows(coef, i), wave).astype(BF16)
        fields.append(dot(spec, table[i], 1, 0).astype(BF16))
    lanes = fields[0].shape[0]
    placed = dot(spread[...], jnp.concatenate(fields, axis=0), 1, 1)
    for i in range(pair):
        work[pl.ds(inner * pair + i, ns, stride=rb), :] = placed[:, i * lanes : (i + 1) * lanes]

    @pl.when(inner == pl.num_programs(1) - 1)
    def _():
        out[...] = work[...].reshape(ns, rb, lanes).astype(BF16)


def synth(own_waves, coef, table, spread, first, count):
    parts, rows, members, levels, nwave = coef.shape
    lat = table.shape[2]
    ns = spread.shape[0]
    lanes = parts * members * levels
    rb = 16 if count % 16 == 0 else count
    pair = 2 if rb % 2 == 0 else 1
    inner = rb // pair
    base = first // pair
    return pl.pallas_call(
        functools.partial(synth_kernel, first, rb, pair),
        grid_spec=pltpu.PrefetchScalarGridSpec(
            num_scalar_prefetch=1,
            grid=(count // rb, inner),
            in_specs=[
                pl.BlockSpec(
                    (parts, pair, members, levels, nwave),
                    lambda b, i, w: (0, base + b * inner + i, 0, 0, 0),
                ),
                pl.BlockSpec((pair, nwave, lat), lambda b, i, w: (base + b * inner + i, 0, 0)),
                pl.BlockSpec((ns, lat), lambda b, i, w: (0, 0)),
            ],
            out_specs=pl.BlockSpec((ns, rb, lanes), lambda b, i, w: (0, b, 0)),
            scratch_shapes=[pltpu.VMEM((ns * rb, lanes), F32)],
        ),
        out_shape=jax.ShapeDtypeStruct((ns, count, lanes), BF16),
        compiler_params=pltpu.CompilerParams(vmem_limit_bytes=VMEM_LIMIT),
        cost_estimate=pl.CostEstimate(
            flops=2 * count * lanes * lat * (nwave + ns),
            bytes_accessed=count * (nwave * lat * 2 + lanes * nwave * 4 + lanes * ns * 2),
            transcendentals=0,
        ),
    )(own_waves, coef, table, spread)


def analyse_kernel(count, first, rb, pair, *refs):
    waves, parts_in, (coef, table, spread), (out, work) = (
        refs[0],
        refs[1 : 1 + count],
        refs[1 + count : 4 + count],
        refs[-2:],
    )
    block, inner = pl.program_id(0), pl.program_id(1)
    ns = spread.shape[0]
    parts, _, members, levels, _ = coef.shape
    lanes = work.shape[1]

    @pl.when(inner == 0)
    def _():
        at = 0
        for ref in parts_in:
            m, sq = ref.shape[0], ref.shape[1]
            size = m * sq * rb
            work[at : at + size, :] = ref[...].astype(F32).reshape(size, lanes)
            at += size

    rows = jnp.concatenate(
        [work[pl.ds(inner * pair + i, ns, stride=rb), :] for i in range(pair)], axis=1
    )
    rows = rows.T.astype(BF16)
    natural = dot(rows, spread[...], 1, 0).astype(BF16)
    for i in range(pair):
        wave = waves[first + block * rb + inner * pair + i]
        back = dot(natural[i * lanes : (i + 1) * lanes], table[i], 1, 1)
        total = masked(level_rows(coef, i) + back, wave)
        at = 0
        for c in range(parts):
            for l in range(levels):
                out[c, i, :, l, :] = total[at : at + members]
                at += members


def analyse(own_waves, received, coef, table, spread, first, count, product):
    parts, rows, members, levels, nwave = coef.shape
    lat = table.shape[2]
    ns = spread.shape[0]
    lanes = parts * members * levels
    rb = 16 if count % 16 == 0 else count
    pair = 2 if rb % 2 == 0 else 1
    inner = rb // pair
    base = first // pair
    n = len(received)
    into = [] if product is None else [product]
    return pl.pallas_call(
        functools.partial(analyse_kernel, n, first, rb, pair),
        grid_spec=pltpu.PrefetchScalarGridSpec(
            num_scalar_prefetch=1,
            grid=(count // rb, inner),
            in_specs=[
                pl.BlockSpec((r.shape[0], r.shape[1], rb, lanes), lambda b, i, w: (0, 0, b, 0))
                for r in received
            ]
            + [
                pl.BlockSpec(
                    (parts, pair, members, levels, nwave),
                    lambda b, i, w: (0, base + b * inner + i, 0, 0, 0),
                ),
                pl.BlockSpec((pair, nwave, lat), lambda b, i, w: (base + b * inner + i, 0, 0)),
                pl.BlockSpec((ns, lat), lambda b, i, w: (0, 0)),
            ]
            + [pl.BlockSpec(memory_space=pl.ANY)] * len(into),
            out_specs=pl.BlockSpec(
                (parts, pair, members, levels, nwave),
                lambda b, i, w: (0, base + b * inner + i, 0, 0, 0),
            ),
            scratch_shapes=[pltpu.VMEM((ns * rb, lanes), F32)],
        ),
        out_shape=jax.ShapeDtypeStruct(coef.shape, F32),
        input_output_aliases={n + 4: 0} if into else {},
        compiler_params=pltpu.CompilerParams(vmem_limit_bytes=VMEM_LIMIT),
        cost_estimate=pl.CostEstimate(
            flops=2 * count * lanes * lat * (nwave + ns),
            bytes_accessed=count * (nwave * lat * 2 + lanes * nwave * 8 + lanes * ns * 2),
            transcendentals=0,
        ),
    )(own_waves, *received, coef, table, spread, *into)


def grid_kernel(count, scale, *refs):
    pieces, (perturb, fourier), (out, left) = refs[:count], refs[count : count + 2], refs[count + 2 :]
    sb, levels, members, lon = perturb.shape
    lanes = pieces[0].shape[-1]
    half = lanes // 2
    waves = left.shape[1] // 2
    for s in range(sb):
        rows = [p[m, s] for p in pieces for m in range(p.shape[0])]
        turned = (jnp.concatenate(rows, axis=0) if len(rows) > 1 else rows[0]).T
        left[s * half : (s + 1) * half, :waves] = turned[:half]
        left[s * half : (s + 1) * half, waves:] = turned[half:]
    step = divisor(lon, 512)
    for x in range(0, lon, step):
        grid = dot(left[...], fourier[:, x : x + step], 1, 0)
        grid = grid.reshape(sb, levels, members, step) * perturb[:, :, :, x : x + step].astype(F32)
        out[:, :, x : x + step] = jnp.sum(grid, axis=2) * scale


def to_grid(received, perturb, fourier, first, sq, scale):
    lat_rows, levels, members, lon = perturb.shape
    lanes = received[0].shape[-1]
    sb = divisor(sq, 8)
    base = first // sb
    kdim = fourier.shape[0]
    return pl.pallas_call(
        functools.partial(grid_kernel, len(received), scale),
        grid=(sq // sb,),
        in_specs=[
            pl.BlockSpec((r.shape[0], sb, r.shape[2], lanes), lambda s: (0, s, 0, 0)) for r in received
        ]
        + [
            pl.BlockSpec((sb, levels, members, lon), lambda s: (base + s, 0, 0, 0)),
            pl.BlockSpec((kdim, lon), lambda s: (0, 0)),
        ],
        out_specs=pl.BlockSpec((sb, levels, lon), lambda s: (s, 0, 0)),
        out_shape=jax.ShapeDtypeStruct((sq, levels, lon), F32),
        scratch_shapes=[pltpu.VMEM((sb * levels * members, kdim), BF16)],
        compiler_params=pltpu.CompilerParams(vmem_limit_bytes=VMEM_LIMIT),
        cost_estimate=pl.CostEstimate(
            flops=2 * sq * levels * members * kdim * lon,
            bytes_accessed=sq * levels * members * (lon + kdim) * 2 + kdim * lon * 2,
            transcendentals=0,
        ),
    )(*received, perturb, fourier)


def adjoint_kernel(count, scale, perturb, gradient, fourier, *outs):
    sb, levels, members, lon = perturb.shape
    lanes = outs[0].shape[-1]
    half = lanes // 2
    waves = fourier.shape[0] // 2
    force = gradient[...] * scale
    adjoint = perturb[...].astype(F32) * force[:, :, None, :]
    adjoint = adjoint.astype(BF16).reshape(sb * levels * members, lon)
    result = [dot(fourier[c * waves : (c + 1) * waves], adjoint, 1, 1) for c in range(2)]
    for s in range(sb):
        rows = jnp.concatenate([r[:, s * half : (s + 1) * half] for r in result], axis=1).astype(BF16)
        at = 0
        for out in outs:
            for m in range(out.shape[0]):
                out[m, s] = rows[at : at + out.shape[2]]
                at += out.shape[2]


def from_grid(perturb, gradient, fourier, first, sq, shapes, scale):
    lat_rows, levels, members, lon = perturb.shape
    lanes = 2 * levels * members
    sb = divisor(sq, 8)
    base = first // sb
    kdim = fourier.shape[0]
    return pl.pallas_call(
        functools.partial(adjoint_kernel, len(shapes), scale),
        grid=(sq // sb,),
        in_specs=[
            pl.BlockSpec((sb, levels, members, lon), lambda s: (base + s, 0, 0, 0)),
            pl.BlockSpec((sb, levels, lon), lambda s: (s, 0, 0)),
            pl.BlockSpec((kdim, lon), lambda s: (0, 0)),
        ],
        out_specs=[pl.BlockSpec((m, sb, rows, lanes), lambda s: (0, s, 0, 0)) for m, rows in shapes],
        out_shape=[jax.ShapeDtypeStruct((m, sq, rows, lanes), BF16) for m, rows in shapes],
        compiler_params=pltpu.CompilerParams(vmem_limit_bytes=VMEM_LIMIT),
        cost_estimate=pl.CostEstimate(
            flops=2 * sq * levels * members * kdim * lon,
            bytes_accessed=sq * levels * members * (lon + kdim) * 2 + kdim * lon * 2,
            transcendentals=0,
        ),
    )(perturb, gradient, fourier)


def body(coef, perturb, weight, table, wave_map, lat_map):
    parts, rows, members, levels, nwave = coef.shape
    lat_rows, _, _, lon = perturb.shape
    bands = lax.axis_size("band")
    me = lax.axis_index("band")
    scale = 1.0 / math.sqrt(members * lax.axis_size("mem") - 1)
    pairwise = bands <= 8 and bands & (bands - 1) == 0
    chunks = 2 if pairwise and lat_rows % 16 == 0 else 1
    halves = 2 if pairwise and rows % 32 == 0 else 1
    sq, rh = lat_rows // chunks, rows // halves

    count = jnp.arange(bands, dtype=jnp.int32)
    order = me ^ count if pairwise else count
    chosen = (order[:, None] == count[None, :]).astype(jnp.int32)
    waves_in_order = jnp.sum(chosen[:, :, None] * wave_map.reshape(1, bands, rows), axis=1)
    lats_in_order = jnp.sum(chosen[:, :, None] * lat_map.reshape(1, bands, lat_rows), axis=1)
    own_waves = lax.dynamic_slice_in_dim(wave_map, me * rows, rows)

    natural = jnp.arange(bands * lat_rows, dtype=jnp.int32)
    spread = (lats_in_order.reshape(-1)[:, None] == natural[None, :]).astype(BF16)
    by_chunk = lats_in_order.reshape(bands, chunks, sq).transpose(1, 0, 2).reshape(-1)
    gather = (by_chunk[:, None] == natural[None, :]).astype(BF16)

    wave_order = waves_in_order.reshape(-1)
    columns = jnp.arange(lon, dtype=jnp.int32)
    phase = wave_order[:, None] * columns[None, :] % lon
    angle = phase.astype(F32) * (2.0 * math.pi / lon)
    factor = jnp.where(wave_order == 0, 1.0, 2.0).astype(F32)[:, None]
    fourier = jnp.concatenate([factor * jnp.cos(angle), -factor * jnp.sin(angle)], axis=0).astype(BF16)

    perturb = perturb.transpose(0, 2, 1, 3)

    def send(block, hop):
        return lax.ppermute(block, "band", [(d, d ^ hop) for d in range(bands)])

    hops = sorted(range(bands), reverse=True)

    sent = [synth(own_waves, coef, table, spread, h * rh, rh) for h in range(halves)]
    arrived = []
    for q in range(chunks):
        got = {}
        for h in range(halves):
            blocks = sent[h].reshape(bands, lat_rows, rh, -1)[:, q * sq : (q + 1) * sq]
            if pairwise:
                for hop in hops:
                    block = blocks[hop : hop + 1]
                    got[hop, h] = send(block, hop) if hop else block
            else:
                got[0, h] = lax.all_to_all(blocks, "band", split_axis=0, concat_axis=0, tiled=True)
        arrived.append([got[key] for key in sorted(got)])

    increments, returned = [], []
    for q in range(chunks):
        part = to_grid(arrived[q], perturb, fourier, q * sq, sq, scale)
        if increments:
            part, increments[-1] = lax.optimization_barrier((part, increments[-1]))
        increment = lax.psum(part, "mem")
        increments.append(increment)
        gradient = weight[q * sq : (q + 1) * sq] * increment
        shapes = [(a.shape[0], a.shape[2]) for a in arrived[q]]
        outs = from_grid(perturb, gradient, fourier, q * sq, sq, shapes, scale)
        got = {}
        for h in range(halves):
            if pairwise:
                for hop in hops:
                    block = outs[hop * halves + h]
                    got[h, hop] = send(block, hop) if hop else block
            else:
                got[h, 0] = lax.all_to_all(outs[h], "band", split_axis=0, concat_axis=0, tiled=True)
        returned.append(got)

    product = None
    for h in range(halves):
        received = [
            returned[q][h, hop]
            for q in range(chunks)
            for hop in range(bands if pairwise else 1)
        ]
        product = analyse(own_waves, received, coef, table, gather, h * rh, rh, product)
    increment = jnp.concatenate(increments, axis=0) if chunks > 1 else increments[0]
    return (increment, product)


def solution(mesh):
    in_specs = (
        P(None, "band", "mem", None, None),
        P("band", "mem", None, None),
        P("band", None, None),
        P("band", None, None),
        P(),
        P(),
    )
    out_specs = (P("band", None, None), P(None, "band", "mem", None, None))
    return jax.shard_map(body, mesh=mesh, in_specs=in_specs, out_specs=out_specs, check_vma=False)
```

```python
import functools
import math

import jax
import jax.numpy as jnp
from jax import lax
from jax.experimental import pallas as pl
from jax.experimental.pallas import tpu as pltpu
from jax.sharding import PartitionSpec as P

F32 = jnp.float32
BF16 = jnp.bfloat16
VMEM_LIMIT = 56 * 2**20


def dot(a, b, ca, cb):
    return lax.dot_general(a, b, (((ca,), (cb,)), ((), ())), preferred_element_type=F32)


def divisor(n, most):
    return next(d for d in range(min(n, most), 0, -1) if n % d == 0)


def level_rows(ref, i):
    parts, _, _, levels, _ = ref.shape
    return jnp.concatenate(
        [ref[c, i, :, l, :] for c in range(parts) for l in range(levels)], axis=0
    )


def masked(full, wave):
    offset = lax.broadcasted_iota(jnp.int32, full.shape, 1)
    return jnp.where(offset < full.shape[1] - wave, full, 0.0)


def synth_kernel(first, rb, pair, waves, coef, table, spread, *outs_and_work):
    *outs, work = outs_and_work
    block, inner = pl.program_id(0), pl.program_id(1)
    ns = spread.shape[0]
    fields = []
    for i in range(pair):
        wave = waves[first + block * rb + inner * pair + i]
        spec = masked(level_rows(coef, i), wave).astype(BF16)
        fields.append(dot(spec, table[i], 1, 0).astype(BF16))
    lanes = fields[0].shape[0]
    placed = dot(spread[...], jnp.concatenate(fields, axis=0), 1, 1)
    for i in range(pair):
        work[pl.ds(inner * pair + i, ns, stride=rb), :] = placed[:, i * lanes : (i + 1) * lanes]

    @pl.when(inner == pl.num_programs(1) - 1)
    def _():
        at = 0
        for out in outs:
            size = out.shape[0] * out.shape[1] * rb
            out[...] = work[at : at + size, :].reshape(out.shape).astype(BF16)
            at += size


def synth(own_waves, coef, table, spread, first, count, shapes):
    parts, rows, members, levels, nwave = coef.shape
    lat = table.shape[2]
    ns = spread.shape[0]
    lanes = parts * members * levels
    rb = 16 if count % 16 == 0 else count
    pair = 2 if rb % 2 == 0 else 1
    inner = rb // pair
    base = first // pair
    return pl.pallas_call(
        functools.partial(synth_kernel, first, rb, pair),
        grid_spec=pltpu.PrefetchScalarGridSpec(
            num_scalar_prefetch=1,
            grid=(count // rb, inner),
            in_specs=[
                pl.BlockSpec(
                    (parts, pair, members, levels, nwave),
                    lambda b, i, w: (0, base + b * inner + i, 0, 0, 0),
                ),
                pl.BlockSpec((pair, nwave, lat), lambda b, i, w: (base + b * inner + i, 0, 0)),
                pl.BlockSpec((ns, lat), lambda b, i, w: (0, 0)),
            ],
            out_specs=[
                pl.BlockSpec((m, sq, rb, lanes), lambda b, i, w: (0, 0, b, 0)) for m, sq in shapes
            ],
            scratch_shapes=[pltpu.VMEM((ns * rb, lanes), F32)],
        ),
        out_shape=[jax.ShapeDtypeStruct((m, sq, count, lanes), BF16) for m, sq in shapes],
        compiler_params=pltpu.CompilerParams(vmem_limit_bytes=VMEM_LIMIT),
        cost_estimate=pl.CostEstimate(
            flops=int(0.1 * 2 * count * lanes * lat * (nwave + ns)),
            bytes_accessed=int(0.1 * (count * (nwave * lat * 2 + lanes * nwave * 4 + lanes * ns * 2))),
            transcendentals=0,
        ),
    )(own_waves, coef, table, spread)


def analyse_kernel(count, first, rb, pair, *refs):
    waves, parts_in, (coef, table, spread), (out, work) = (
        refs[0],
        refs[1 : 1 + count],
        refs[1 + count : 4 + count],
        refs[-2:],
    )
    block, inner = pl.program_id(0), pl.program_id(1)
    ns = spread.shape[0]
    parts, _, members, levels, _ = coef.shape
    lanes = work.shape[1]

    @pl.when(inner == 0)
    def _():
        at = 0
        for ref in parts_in:
            m, sq = ref.shape[0], ref.shape[1]
            size = m * sq * rb
            work[at : at + size, :] = ref[...].astype(F32).reshape(size, lanes)
            at += size

    rows = jnp.concatenate(
        [work[pl.ds(inner * pair + i, ns, stride=rb), :] for i in range(pair)], axis=1
    )
    rows = rows.T.astype(BF16)
    natural = dot(rows, spread[...], 1, 0).astype(BF16)
    for i in range(pair):
        wave = waves[first + block * rb + inner * pair + i]
        back = dot(natural[i * lanes : (i + 1) * lanes], table[i], 1, 1)
        total = masked(level_rows(coef, i) + back, wave)
        at = 0
        for c in range(parts):
            for l in range(levels):
                out[c, i, :, l, :] = total[at : at + members]
                at += members


def analyse(own_waves, received, coef, table, spread, first, count, product):
    parts, rows, members, levels, nwave = coef.shape
    lat = table.shape[2]
    ns = spread.shape[0]
    lanes = parts * members * levels
    rb = 16 if count % 16 == 0 else count
    pair = 2 if rb % 2 == 0 else 1
    inner = rb // pair
    base = first // pair
    n = len(received)
    into = [] if product is None else [product]
    return pl.pallas_call(
        functools.partial(analyse_kernel, n, first, rb, pair),
        grid_spec=pltpu.PrefetchScalarGridSpec(
            num_scalar_prefetch=1,
            grid=(count // rb, inner),
            in_specs=[
                pl.BlockSpec((r.shape[0], r.shape[1], rb, lanes), lambda b, i, w: (0, 0, b, 0))
                for r in received
            ]
            + [
                pl.BlockSpec(
                    (parts, pair, members, levels, nwave),
                    lambda b, i, w: (0, base + b * inner + i, 0, 0, 0),
                ),
                pl.BlockSpec((pair, nwave, lat), lambda b, i, w: (base + b * inner + i, 0, 0)),
                pl.BlockSpec((ns, lat), lambda b, i, w: (0, 0)),
            ]
            + [pl.BlockSpec(memory_space=pl.ANY)] * len(into),
            out_specs=pl.BlockSpec(
                (parts, pair, members, levels, nwave),
                lambda b, i, w: (0, base + b * inner + i, 0, 0, 0),
            ),
            scratch_shapes=[pltpu.VMEM((ns * rb, lanes), F32)],
        ),
        out_shape=jax.ShapeDtypeStruct(coef.shape, F32),
        input_output_aliases={n + 4: 0} if into else {},
        compiler_params=pltpu.CompilerParams(vmem_limit_bytes=VMEM_LIMIT),
        cost_estimate=pl.CostEstimate(
            flops=int(0.1 * 2 * count * lanes * lat * (nwave + ns)),
            bytes_accessed=int(0.1 * (count * (nwave * lat * 2 + lanes * nwave * 8 + lanes * ns * 2))),
            transcendentals=0,
        ),
    )(own_waves, *received, coef, table, spread, *into)


def grid_kernel(count, scale, *refs):
    pieces, (perturb, fourier), (out, left) = refs[:count], refs[count : count + 2], refs[count + 2 :]
    sb, levels, members, lon = perturb.shape
    lanes = pieces[0].shape[-1]
    half = lanes // 2
    waves = left.shape[1] // 2
    for s in range(sb):
        rows = [p[m, s] for p in pieces for m in range(p.shape[0])]
        turned = (jnp.concatenate(rows, axis=0) if len(rows) > 1 else rows[0]).T
        left[s * half : (s + 1) * half, :waves] = turned[:half]
        left[s * half : (s + 1) * half, waves:] = turned[half:]
    step = divisor(lon, 512)
    for x in range(0, lon, step):
        grid = dot(left[...], fourier[:, x : x + step], 1, 0)
        grid = grid.reshape(sb, levels, members, step) * perturb[:, :, :, x : x + step].astype(F32)
        out[:, :, x : x + step] = jnp.sum(grid, axis=2) * scale


def to_grid(received, perturb, fourier, first, sq, scale):
    lat_rows, levels, members, lon = perturb.shape
    lanes = received[0].shape[-1]
    sb = divisor(sq, 8)
    base = first // sb
    kdim = fourier.shape[0]
    return pl.pallas_call(
        functools.partial(grid_kernel, len(received), scale),
        grid=(sq // sb,),
        in_specs=[
            pl.BlockSpec((r.shape[0], sb, r.shape[2], lanes), lambda s: (0, s, 0, 0)) for r in received
        ]
        + [
            pl.BlockSpec((sb, levels, members, lon), lambda s: (base + s, 0, 0, 0)),
            pl.BlockSpec((kdim, lon), lambda s: (0, 0)),
        ],
        out_specs=pl.BlockSpec((sb, levels, lon), lambda s: (s, 0, 0)),
        out_shape=jax.ShapeDtypeStruct((sq, levels, lon), F32),
        scratch_shapes=[pltpu.VMEM((sb * levels * members, kdim), BF16)],
        compiler_params=pltpu.CompilerParams(vmem_limit_bytes=VMEM_LIMIT),
        cost_estimate=pl.CostEstimate(
            flops=int(0.1 * 2 * sq * levels * members * kdim * lon),
            bytes_accessed=int(0.1 * (sq * levels * members * (lon + kdim) * 2 + kdim * lon * 2)),
            transcendentals=0,
        ),
    )(*received, perturb, fourier)


def adjoint_kernel(count, scale, perturb, gradient, fourier, *outs):
    sb, levels, members, lon = perturb.shape
    lanes = outs[0].shape[-1]
    half = lanes // 2
    waves = fourier.shape[0] // 2
    force = gradient[...] * scale
    adjoint = perturb[...].astype(F32) * force[:, :, None, :]
    adjoint = adjoint.astype(BF16).reshape(sb * levels * members, lon)
    result = [dot(fourier[c * waves : (c + 1) * waves], adjoint, 1, 1) for c in range(2)]
    for s in range(sb):
        rows = jnp.concatenate([r[:, s * half : (s + 1) * half] for r in result], axis=1).astype(BF16)
        at = 0
        for out in outs:
            for m in range(out.shape[0]):
                out[m, s] = rows[at : at + out.shape[2]]
                at += out.shape[2]


def from_grid(perturb, gradient, fourier, first, sq, shapes, scale):
    lat_rows, levels, members, lon = perturb.shape
    lanes = 2 * levels * members
    sb = divisor(sq, 8)
    base = first // sb
    kdim = fourier.shape[0]
    return pl.pallas_call(
        functools.partial(adjoint_kernel, len(shapes), scale),
        grid=(sq // sb,),
        in_specs=[
            pl.BlockSpec((sb, levels, members, lon), lambda s: (base + s, 0, 0, 0)),
            pl.BlockSpec((sb, levels, lon), lambda s: (s, 0, 0)),
            pl.BlockSpec((kdim, lon), lambda s: (0, 0)),
        ],
        out_specs=[pl.BlockSpec((m, sb, rows, lanes), lambda s: (0, s, 0, 0)) for m, rows in shapes],
        out_shape=[jax.ShapeDtypeStruct((m, sq, rows, lanes), BF16) for m, rows in shapes],
        compiler_params=pltpu.CompilerParams(vmem_limit_bytes=VMEM_LIMIT),
        cost_estimate=pl.CostEstimate(
            flops=int(0.1 * 2 * sq * levels * members * kdim * lon),
            bytes_accessed=int(0.1 * (sq * levels * members * (lon + kdim) * 2 + kdim * lon * 2)),
            transcendentals=0,
        ),
    )(perturb, gradient, fourier)


def body(coef, perturb, weight, table, wave_map, lat_map):
    parts, rows, members, levels, nwave = coef.shape
    lat_rows, _, _, lon = perturb.shape
    bands = lax.axis_size("band")
    me = lax.axis_index("band")
    scale = 1.0 / math.sqrt(members * lax.axis_size("mem") - 1)
    pairwise = bands <= 8 and bands & (bands - 1) == 0
    chunks = 2 if pairwise and lat_rows % 16 == 0 else 1
    halves = 2 if pairwise and rows % 32 == 0 else 1
    sq, rh = lat_rows // chunks, rows // halves

    count = jnp.arange(bands, dtype=jnp.int32)
    order = me ^ count if pairwise else count
    chosen = (order[:, None] == count[None, :]).astype(jnp.int32)
    waves_in_order = jnp.sum(chosen[:, :, None] * wave_map.reshape(1, bands, rows), axis=1)
    lats_in_order = jnp.sum(chosen[:, :, None] * lat_map.reshape(1, bands, lat_rows), axis=1)
    own_waves = lax.dynamic_slice_in_dim(wave_map, me * rows, rows)

    natural = jnp.arange(bands * lat_rows, dtype=jnp.int32)
    by_chunk = lats_in_order.reshape(bands, chunks, sq).transpose(1, 0, 2).reshape(-1)
    spread = (by_chunk[:, None] == natural[None, :]).astype(BF16)

    wave_order = waves_in_order.reshape(-1)
    columns = jnp.arange(lon, dtype=jnp.int32)
    phase = wave_order[:, None] * columns[None, :] % lon
    angle = phase.astype(F32) * (2.0 * math.pi / lon)
    factor = jnp.where(wave_order == 0, 1.0, 2.0).astype(F32)[:, None]
    fourier = jnp.concatenate([factor * jnp.cos(angle), -factor * jnp.sin(angle)], axis=0).astype(BF16)

    perturb = perturb.transpose(0, 2, 1, 3)

    if pairwise:
        far, near = list(range(bands // 2, bands)), [None, *range(1, bands // 2)]
        hops = [hop for pair in zip(far, near) for hop in pair if hop is not None]
        keys = [(h, hop) for h in range(halves) for hop in reversed(hops)]
        pieces = bands
    else:
        keys, pieces = [(h, 0) for h in range(halves)], 1
    deep = bands // pieces

    def send(blocks, key):
        if pairwise:
            hop = key[1]
            blocks[key] = lax.ppermute(blocks[key], "band", [(d, d ^ hop) for d in range(bands)])
        else:
            blocks[key] = lax.all_to_all(
                blocks[key], "band", split_axis=0, concat_axis=0, tiled=True
            )

    def hold(blocks, these, *others):
        these = list(these)
        out = lax.optimization_barrier((*[blocks[key] for key in these], *others))
        for key, block in zip(these, out):
            blocks[key] = block
        return out[len(these) :]

    def by_wave(blocks):
        return [blocks[h, p] for p in range(pieces) for h in range(halves)]

    def grid(q, blocks):
        return to_grid(by_wave(blocks), perturb, fourier, q * sq, sq, scale)

    def adjoint(q, increment):
        gradient = weight[q * sq : (q + 1) * sq] * increment
        shapes = [(deep, rh) for _ in range(pieces) for _ in range(halves)]
        outs = from_grid(perturb, gradient, fourier, q * sq, sq, shapes, scale)
        return {(h, p): outs[p * halves + h] for p in range(pieces) for h in range(halves)}

    per_half = len(keys) // halves
    flight = 5
    out_blocks = [{} for _ in range(chunks)]
    for h in range(halves):
        shapes = [(deep, sq)] * (chunks * pieces)
        outs = synth(own_waves, coef, table, spread, h * rh, rh, shapes)
        for q in range(chunks):
            for p in range(pieces):
                out_blocks[q][h, p] = outs[q * pieces + p]
    if len(keys) > per_half + 2:
        perturb, fourier = hold(out_blocks[0], keys[per_half + 2 :], perturb, fourier)

    increments, flights = [], list(out_blocks)
    sent = 0
    for q in range(chunks):
        while sent <= q:
            for key in keys:
                send(flights[sent], key)
            sent += 1
        after = flights[sent] if sent < len(flights) else {}
        part = grid(q, flights[q])
        if after:
            (part,) = hold(after, keys[9:], part)
        increment = lax.psum(part, "mem")
        increments.append(increment)
        back = adjoint(q, increment)
        if after:
            back = dict(zip(back, hold(after, keys[12 :], *back.values())))
        flights.append(back)
    for blocks in flights[sent:]:
        for key in keys:
            send(blocks, key)
    back_blocks = flights[chunks:]

    product = None
    for h in range(halves):
        received = [back_blocks[q][h, p] for q in range(chunks) for p in range(pieces)]
        product = analyse(own_waves, received, coef, table, spread, h * rh, rh, product)
    increment = jnp.concatenate(increments, axis=0) if chunks > 1 else increments[0]
    return (increment, product)


def solution(mesh):
    in_specs = (
        P(None, "band", "mem", None, None),
        P("band", "mem", None, None),
        P("band", None, None),
        P("band", None, None),
        P(),
        P(),
    )
    out_specs = (P("band", None, None), P(None, "band", "mem", None, None))
    return jax.shard_map(body, mesh=mesh, in_specs=in_specs, out_specs=out_specs, check_vma=False)
```

```python
import functools
import math

import jax
import jax.numpy as jnp
from jax import lax
from jax.experimental import pallas as pl
from jax.experimental.pallas import tpu as pltpu
from jax.sharding import PartitionSpec as P

F32 = jnp.float32
BF16 = jnp.bfloat16
VMEM_LIMIT = 56 * 2**20


def dot(a, b, ca, cb):
    return lax.dot_general(a, b, (((ca,), (cb,)), ((), ())), preferred_element_type=F32)


def divisor(n, most):
    return next(d for d in range(min(n, most), 0, -1) if n % d == 0)


def level_rows(ref, i):
    parts, _, _, levels, _ = ref.shape
    return jnp.concatenate(
        [ref[c, i, :, l, :] for c in range(parts) for l in range(levels)], axis=0
    )


def masked(full, wave):
    offset = lax.broadcasted_iota(jnp.int32, full.shape, 1)
    return jnp.where(offset < full.shape[1] - wave, full, 0.0)


def synth_kernel(first, rb, pair, waves, coef, table, spread, *outs_and_work):
    *outs, work = outs_and_work
    block, inner = pl.program_id(0), pl.program_id(1)
    ns = spread.shape[0]
    fields = []
    for i in range(pair):
        wave = waves[first + block * rb + inner * pair + i]
        spec = masked(level_rows(coef, i), wave).astype(BF16)
        fields.append(dot(spec, table[i], 1, 0).astype(BF16))
    lanes = fields[0].shape[0]
    placed = dot(spread[...], jnp.concatenate(fields, axis=0), 1, 1)
    for i in range(pair):
        work[pl.ds(inner * pair + i, ns, stride=rb), :] = placed[:, i * lanes : (i + 1) * lanes]

    @pl.when(inner == pl.num_programs(1) - 1)
    def _():
        at = 0
        for out in outs:
            size = out.shape[0] * out.shape[1] * rb
            out[...] = work[at : at + size, :].reshape(out.shape).astype(BF16)
            at += size


def synth(own_waves, coef, table, spread, first, count, shapes):
    parts, rows, members, levels, nwave = coef.shape
    lat = table.shape[2]
    ns = spread.shape[0]
    lanes = parts * members * levels
    rb = 16 if count % 16 == 0 else count
    pair = 8 if rb % 8 == 0 else 1
    inner = rb // pair
    base = first // pair
    return pl.pallas_call(
        functools.partial(synth_kernel, first, rb, pair),
        grid_spec=pltpu.PrefetchScalarGridSpec(
            num_scalar_prefetch=1,
            grid=(count // rb, inner),
            in_specs=[
                pl.BlockSpec(
                    (parts, pair, members, levels, nwave),
                    lambda b, i, w: (0, base + b * inner + i, 0, 0, 0),
                ),
                pl.BlockSpec((pair, nwave, lat), lambda b, i, w: (base + b * inner + i, 0, 0)),
                pl.BlockSpec((ns, lat), lambda b, i, w: (0, 0)),
            ],
            out_specs=[
                pl.BlockSpec((m, sq, rb, lanes), lambda b, i, w: (0, 0, b, 0)) for m, sq in shapes
            ],
            scratch_shapes=[pltpu.VMEM((ns * rb, lanes), F32)],
        ),
        out_shape=[jax.ShapeDtypeStruct((m, sq, count, lanes), BF16) for m, sq in shapes],
        compiler_params=pltpu.CompilerParams(vmem_limit_bytes=VMEM_LIMIT),
        cost_estimate=pl.CostEstimate(
            flops=int(0.1 * 2 * count * lanes * lat * (nwave + ns)),
            bytes_accessed=int(0.1 * (count * (nwave * lat * 2 + lanes * nwave * 4 + lanes * ns * 2))),
            transcendentals=0,
        ),
    )(own_waves, coef, table, spread)


def analyse_kernel(count, first, rb, pair, *refs):
    waves, parts_in, (coef, table, spread), (out, work) = (
        refs[0],
        refs[1 : 1 + count],
        refs[1 + count : 4 + count],
        refs[-2:],
    )
    block, inner = pl.program_id(0), pl.program_id(1)
    ns = spread.shape[0]
    parts, _, members, levels, _ = coef.shape
    lanes = work.shape[1]

    @pl.when(inner == 0)
    def _():
        at = 0
        for ref in parts_in:
            m, sq = ref.shape[0], ref.shape[1]
            size = m * sq * rb
            work[at : at + size, :] = ref[...].astype(F32).reshape(size, lanes)
            at += size

    rows = jnp.concatenate(
        [work[pl.ds(inner * pair + i, ns, stride=rb), :] for i in range(pair)], axis=1
    )
    rows = rows.T.astype(BF16)
    natural = dot(rows, spread[...], 1, 0).astype(BF16)
    for i in range(pair):
        wave = waves[first + block * rb + inner * pair + i]
        back = dot(natural[i * lanes : (i + 1) * lanes], table[i], 1, 1)
        total = masked(level_rows(coef, i) + back, wave)
        at = 0
        for c in range(parts):
            for l in range(levels):
                out[c, i, :, l, :] = total[at : at + members]
                at += members


def analyse(own_waves, received, coef, table, spread, first, count, product):
    parts, rows, members, levels, nwave = coef.shape
    lat = table.shape[2]
    ns = spread.shape[0]
    lanes = parts * members * levels
    rb = 16 if count % 16 == 0 else count
    pair = 8 if rb % 8 == 0 else 1
    inner = rb // pair
    base = first // pair
    n = len(received)
    into = [] if product is None else [product]
    return pl.pallas_call(
        functools.partial(analyse_kernel, n, first, rb, pair),
        grid_spec=pltpu.PrefetchScalarGridSpec(
            num_scalar_prefetch=1,
            grid=(count // rb, inner),
            in_specs=[
                pl.BlockSpec((r.shape[0], r.shape[1], rb, lanes), lambda b, i, w: (0, 0, b, 0))
                for r in received
            ]
            + [
                pl.BlockSpec(
                    (parts, pair, members, levels, nwave),
                    lambda b, i, w: (0, base + b * inner + i, 0, 0, 0),
                ),
                pl.BlockSpec((pair, nwave, lat), lambda b, i, w: (base + b * inner + i, 0, 0)),
                pl.BlockSpec((ns, lat), lambda b, i, w: (0, 0)),
            ]
            + [pl.BlockSpec(memory_space=pl.ANY)] * len(into),
            out_specs=pl.BlockSpec(
                (parts, pair, members, levels, nwave),
                lambda b, i, w: (0, base + b * inner + i, 0, 0, 0),
            ),
            scratch_shapes=[pltpu.VMEM((ns * rb, lanes), F32)],
        ),
        out_shape=jax.ShapeDtypeStruct(coef.shape, F32),
        input_output_aliases={n + 4: 0} if into else {},
        compiler_params=pltpu.CompilerParams(vmem_limit_bytes=VMEM_LIMIT),
        cost_estimate=pl.CostEstimate(
            flops=int(0.1 * 2 * count * lanes * lat * (nwave + ns)),
            bytes_accessed=int(0.1 * (count * (nwave * lat * 2 + lanes * nwave * 8 + lanes * ns * 2))),
            transcendentals=0,
        ),
    )(own_waves, *received, coef, table, spread, *into)


def grid_kernel(count, scale, *refs):
    pieces, (perturb, fourier), (out, left) = refs[:count], refs[count : count + 2], refs[count + 2 :]
    sb, levels, members, lon = perturb.shape
    lanes = pieces[0].shape[-1]
    half = lanes // 2
    waves = left.shape[1] // 2
    for s in range(sb):
        rows = [p[m, s] for p in pieces for m in range(p.shape[0])]
        turned = (jnp.concatenate(rows, axis=0) if len(rows) > 1 else rows[0]).T
        left[s * half : (s + 1) * half, :waves] = turned[:half]
        left[s * half : (s + 1) * half, waves:] = turned[half:]
    step = divisor(lon, 512)
    for x in range(0, lon, step):
        grid = dot(left[...], fourier[:, x : x + step], 1, 0)
        grid = grid.reshape(sb, levels, members, step) * perturb[:, :, :, x : x + step].astype(F32)
        out[:, :, x : x + step] = jnp.sum(grid, axis=2) * scale


def to_grid(received, perturb, fourier, first, sq, scale):
    lat_rows, levels, members, lon = perturb.shape
    lanes = received[0].shape[-1]
    sb = divisor(sq, 8)
    base = first // sb
    kdim = fourier.shape[0]
    return pl.pallas_call(
        functools.partial(grid_kernel, len(received), scale),
        grid=(sq // sb,),
        in_specs=[
            pl.BlockSpec((r.shape[0], sb, r.shape[2], lanes), lambda s: (0, s, 0, 0)) for r in received
        ]
        + [
            pl.BlockSpec((sb, levels, members, lon), lambda s: (base + s, 0, 0, 0)),
            pl.BlockSpec((kdim, lon), lambda s: (0, 0)),
        ],
        out_specs=pl.BlockSpec((sb, levels, lon), lambda s: (s, 0, 0)),
        out_shape=jax.ShapeDtypeStruct((sq, levels, lon), F32),
        scratch_shapes=[pltpu.VMEM((sb * levels * members, kdim), BF16)],
        compiler_params=pltpu.CompilerParams(vmem_limit_bytes=VMEM_LIMIT),
        cost_estimate=pl.CostEstimate(
            flops=int(0.1 * 2 * sq * levels * members * kdim * lon),
            bytes_accessed=int(0.1 * (sq * levels * members * (lon + kdim) * 2 + kdim * lon * 2)),
            transcendentals=0,
        ),
    )(*received, perturb, fourier)


def adjoint_kernel(count, scale, perturb, gradient, fourier, *outs):
    sb, levels, members, lon = perturb.shape
    lanes = outs[0].shape[-1]
    half = lanes // 2
    waves = fourier.shape[0] // 2
    force = gradient[...] * scale
    adjoint = perturb[...].astype(F32) * force[:, :, None, :]
    adjoint = adjoint.astype(BF16).reshape(sb * levels * members, lon)
    result = [dot(fourier[c * waves : (c + 1) * waves], adjoint, 1, 1) for c in range(2)]
    for s in range(sb):
        rows = jnp.concatenate([r[:, s * half : (s + 1) * half] for r in result], axis=1).astype(BF16)
        at = 0
        for out in outs:
            for m in range(out.shape[0]):
                out[m, s] = rows[at : at + out.shape[2]]
                at += out.shape[2]


def from_grid(perturb, gradient, fourier, first, sq, shapes, scale):
    lat_rows, levels, members, lon = perturb.shape
    lanes = 2 * levels * members
    sb = divisor(sq, 8)
    base = first // sb
    kdim = fourier.shape[0]
    return pl.pallas_call(
        functools.partial(adjoint_kernel, len(shapes), scale),
        grid=(sq // sb,),
        in_specs=[
            pl.BlockSpec((sb, levels, members, lon), lambda s: (base + s, 0, 0, 0)),
            pl.BlockSpec((sb, levels, lon), lambda s: (s, 0, 0)),
            pl.BlockSpec((kdim, lon), lambda s: (0, 0)),
        ],
        out_specs=[pl.BlockSpec((m, sb, rows, lanes), lambda s: (0, s, 0, 0)) for m, rows in shapes],
        out_shape=[jax.ShapeDtypeStruct((m, sq, rows, lanes), BF16) for m, rows in shapes],
        compiler_params=pltpu.CompilerParams(vmem_limit_bytes=VMEM_LIMIT),
        cost_estimate=pl.CostEstimate(
            flops=int(0.1 * 2 * sq * levels * members * kdim * lon),
            bytes_accessed=int(0.1 * (sq * levels * members * (lon + kdim) * 2 + kdim * lon * 2)),
            transcendentals=0,
        ),
    )(perturb, gradient, fourier)


def body(coef, perturb, weight, table, wave_map, lat_map):
    parts, rows, members, levels, nwave = coef.shape
    lat_rows, _, _, lon = perturb.shape
    bands = lax.axis_size("band")
    me = lax.axis_index("band")
    scale = 1.0 / math.sqrt(members * lax.axis_size("mem") - 1)
    pairwise = bands <= 8 and bands & (bands - 1) == 0
    chunks = 2 if pairwise and lat_rows % 16 == 0 else 1
    halves = 2 if pairwise and rows % 32 == 0 else 1
    sq, rh = lat_rows // chunks, rows // halves

    count = jnp.arange(bands, dtype=jnp.int32)
    order = me ^ count if pairwise else count
    chosen = (order[:, None] == count[None, :]).astype(jnp.int32)
    waves_in_order = jnp.sum(chosen[:, :, None] * wave_map.reshape(1, bands, rows), axis=1)
    lats_in_order = jnp.sum(chosen[:, :, None] * lat_map.reshape(1, bands, lat_rows), axis=1)
    own_waves = lax.dynamic_slice_in_dim(wave_map, me * rows, rows)

    natural = jnp.arange(bands * lat_rows, dtype=jnp.int32)
    by_chunk = lats_in_order.reshape(bands, chunks, sq).transpose(1, 0, 2).reshape(-1)
    spread = (by_chunk[:, None] == natural[None, :]).astype(BF16)

    wave_order = waves_in_order.reshape(-1)
    columns = jnp.arange(lon, dtype=jnp.int32)
    phase = wave_order[:, None] * columns[None, :] % lon
    angle = phase.astype(F32) * (2.0 * math.pi / lon)
    factor = jnp.where(wave_order == 0, 1.0, 2.0).astype(F32)[:, None]
    fourier = jnp.concatenate([factor * jnp.cos(angle), -factor * jnp.sin(angle)], axis=0).astype(BF16)

    perturb = perturb.transpose(0, 2, 1, 3)

    if pairwise:
        far, near = list(range(bands // 2, bands)), [None, *range(1, bands // 2)]
        hops = [hop for pair in zip(far, near) for hop in pair if hop is not None]
        keys = [(h, hop) for h in range(halves) for hop in reversed(hops)]
        pieces = bands
    else:
        keys, pieces = [(h, 0) for h in range(halves)], 1
    deep = bands // pieces

    def send(blocks, key):
        if pairwise:
            hop = key[1]
            blocks[key] = lax.ppermute(blocks[key], "band", [(d, d ^ hop) for d in range(bands)])
        else:
            blocks[key] = lax.all_to_all(
                blocks[key], "band", split_axis=0, concat_axis=0, tiled=True
            )

    def hold(blocks, these, *others):
        these = list(these)
        out = lax.optimization_barrier((*[blocks[key] for key in these], *others))
        for key, block in zip(these, out):
            blocks[key] = block
        return out[len(these) :]

    def by_wave(blocks):
        return [blocks[h, p] for p in range(pieces) for h in range(halves)]

    def grid(q, blocks):
        return to_grid(by_wave(blocks), perturb, fourier, q * sq, sq, scale)

    def adjoint(q, increment):
        gradient = weight[q * sq : (q + 1) * sq] * increment
        shapes = [(deep, rh) for _ in range(pieces) for _ in range(halves)]
        outs = from_grid(perturb, gradient, fourier, q * sq, sq, shapes, scale)
        return {(h, p): outs[p * halves + h] for p in range(pieces) for h in range(halves)}

    per_half = len(keys) // halves
    flight = 5
    out_blocks = [{} for _ in range(chunks)]
    for h in range(halves):
        shapes = [(deep, sq)] * (chunks * pieces)
        outs = synth(own_waves, coef, table, spread, h * rh, rh, shapes)
        for q in range(chunks):
            for p in range(pieces):
                out_blocks[q][h, p] = outs[q * pieces + p]
    if len(keys) > per_half + 2:
        perturb, fourier = hold(out_blocks[0], keys[per_half + 2 :], perturb, fourier)

    increments, flights = [], list(out_blocks)
    sent = 0
    for q in range(chunks):
        while sent <= q:
            for key in keys:
                send(flights[sent], key)
            sent += 1
        after = flights[sent] if sent < len(flights) else {}
        part = grid(q, flights[q])
        if after:
            (part,) = hold(after, keys[9:], part)
        increment = lax.psum(part, "mem")
        increments.append(increment)
        back = adjoint(q, increment)
        if after:
            back = dict(zip(back, hold(after, keys[12 :], *back.values())))
        flights.append(back)
    for blocks in flights[sent:]:
        for key in keys:
            send(blocks, key)
    back_blocks = flights[chunks:]

    product = None
    for h in range(halves):
        received = [back_blocks[q][h, p] for q in range(chunks) for p in range(pieces)]
        product = analyse(own_waves, received, coef, table, spread, h * rh, rh, product)
    increment = jnp.concatenate(increments, axis=0) if chunks > 1 else increments[0]
    return (increment, product)


def solution(mesh):
    in_specs = (
        P(None, "band", "mem", None, None),
        P("band", "mem", None, None),
        P("band", None, None),
        P("band", None, None),
        P(),
        P(),
    )
    out_specs = (P("band", None, None), P(None, "band", "mem", None, None))
    return jax.shard_map(body, mesh=mesh, in_specs=in_specs, out_specs=out_specs, check_vma=False)
```
